128 devices in a mesh: fsdp: 16 (over z_hi, y, core), refresh: 8 (over z_lo, x).
Axes of the slice: x: 4, y: 4, z: 4 (z_hi: 2, z_lo: 2; z = z_hi * 2 + z_lo), core: 2. Of those that a mesh axis runs over, the one named last changes fastest.
Arguments:
- grad: bfloat16 [4096, 4096], P('fsdp', 'refresh'), may hold values from -6 to 6
- exp_avg: float32 [4096, 4096], P('fsdp', 'refresh'), may hold values from -1.75 to 1.75
- exp_avg_sq: float32 [4096, 4096], P('fsdp', 'refresh'), may hold values from 0.01 to 1
- left_codes: int32 [4096, 4096], P('fsdp'), may hold values from 0 to 15
- left_scales: float32 [4096, 32], P('fsdp'), may hold values from 0.001953125 to 0.005
- right_old_codes: int32 [4096, 4096], P('refresh'), may hold values from 0 to 15
- right_old_scales: float32 [4096, 32], P('refresh'), may hold values from 0.001953125 to 0.005
- right_new_codes: int32 [4096, 4096], P('refresh'), may hold values from 0 to 15
- right_new_scales: float32 [4096, 32], P('refresh'), may hold values from 0.001953125 to 0.005
Outputs:
- new_exp_avg: float32 [4096, 4096], P('fsdp', 'refresh')
- new_exp_avg_sq: float32 [4096, 4096], P('fsdp', 'refresh')
- update: float32 [4096, 4096], P('fsdp', 'refresh')
The draws below stay inside these ranges and needn't reach their ends.
All inputs are finite; a program needn't handle non-finite values.
Results may differ from the reference program's by a relative error of at most 0.0054.
Values may be sent and summed in bfloat16 or wider, within the bound.
A program may use at most 128 MiB of HBM per device.

```python
import math
import jax
import jax.numpy as jnp
from jax import lax

B = 4096
QG = 128
STEP = 20


def paired_codes(key):
    first_key, second_key, third_key = jax.random.split(key, 3)
    base = jax.random.randint(first_key, (B, B), 0, 16, dtype=jnp.int32)
    fresh = jax.random.randint(second_key, (B, B), 0, 16, dtype=jnp.int32)
    kept = jax.random.randint(third_key, (B, B), 0, 2, dtype=jnp.int32)
    return (base, jnp.where(kept == 1, base, fresh))


def draw_right_old_codes(key, part):
    return paired_codes(key)[0]


def draw_right_new_codes(key, part):
    return paired_codes(key)[1]


def touch_ends(entries, rng, smallest, largest):
    index_at = [jax.random.randint(jax.random.fold_in(rng, axis), (), 0, length) for axis, length in enumerate(entries.shape)]
    main_axis = entries.shape.index(max(entries.shape))
    beside = index_at[:main_axis] + [(index_at[main_axis] + 1) % entries.shape[main_axis]] + index_at[main_axis + 1:]
    return entries.at[tuple(index_at)].set(smallest).at[tuple(beside)].set(largest)


def steps_of(rng, extent, pieces, smallest, high):
    gain, own = 1.0, jax.random.fold_in(rng, 6)
    for axis_at, shards_of in pieces:
        steps = jnp.exp(jax.random.uniform(jax.random.fold_in(own, axis_at), (shards_of,), jnp.float32, smallest / len(pieces), high / len(pieces)))
        gain = gain * jnp.repeat(steps, extent[axis_at] // shards_of).reshape([-1 if axis == axis_at else 1 for axis in range(len(extent))])
    return gain


def gaussian(key, dims, scale, bound, cuts=(), kind=jnp.bfloat16):
    loudness = steps_of(key, dims, cuts, -0.22, 0.18) if cuts else 1.0
    drawn = jax.random.normal(key, dims, jnp.float32) * scale * loudness
    return jnp.minimum(jnp.maximum(drawn, -bound), bound).astype(kind)


def setup_inputs(seed: int = 0) -> dict:
    seeds = jax.random.split(jax.random.key(seed), 10)
    return {
        "grad": gaussian(seeds[0], (B, B), 1.0, 6.0, ((0, 16), (1, 8))),
        "exp_avg": gaussian(seeds[1], (B, B), 0.3, 1.75, ((0, 16), (1, 8)), jnp.float32),
        "exp_avg_sq": jnp.clip(jnp.exp(math.log(1.0) - 4.6051702 * jax.random.uniform(seeds[2], (B, B), jnp.float32) ** steps_of(seeds[2], (B, B), ((0, 16), (1, 8)), -0.2, 0.2)), 0.01, 1.0),
        "left_codes": touch_ends(jax.random.randint(seeds[3], (B, B), 0, 16), jax.random.fold_in(seeds[3], 1), 0, 15).astype(jnp.int32),
        "left_scales": jnp.clip(jnp.exp(math.log(0.005) - 0.9400072 * jax.random.uniform(seeds[4], (B, B // QG), jnp.float32) ** steps_of(seeds[4], (B, B // QG), ((0, 16),), -0.2, 0.2)), 0.001953125, 0.005),
        "right_old_codes": draw_right_old_codes(jax.random.fold_in(seeds[9], 71), 0),
        "right_old_scales": jnp.clip(jnp.exp(math.log(0.005) - 0.9400072 * jax.random.uniform(seeds[6], (B, B // QG), jnp.float32) ** steps_of(seeds[6], (B, B // QG), ((0, 8),), -0.2, 0.2)), 0.001953125, 0.005),
        "right_new_codes": draw_right_new_codes(jax.random.fold_in(seeds[9], 71), 0),
        "right_new_scales": jnp.clip(jnp.exp(math.log(0.005) - 0.9400072 * jax.random.uniform(seeds[8], (B, B // QG), jnp.float32) ** steps_of(seeds[8], (B, B // QG), ((0, 8),), -0.2, 0.2)), 0.001953125, 0.005),
    }


first_beta = 0.9
second_beta = 0.95
epsilon = 1e-08

def dequantize(codes, scales):
    groups = codes.shape[1] // scales.shape[1]
    levels = codes.astype(jnp.float32) - 7.5
    widened = jnp.repeat(scales, groups, axis=1)
    return (levels * widened).astype(jnp.bfloat16)

def reference(grad, exp_avg, exp_avg_sq, left_codes, left_scales, right_old_codes, right_old_scales, right_new_codes, right_new_scales):
    left_basis = dequantize(left_codes, left_scales)
    old_basis = dequantize(right_old_codes, right_old_scales)
    new_basis = dequantize(right_new_codes, right_new_scales)
    transition = jnp.dot(old_basis.T, new_basis, preferred_element_type=jnp.float32)
    first_moment = jnp.dot(exp_avg, transition, precision=lax.Precision.HIGHEST)
    second_moment = jnp.dot(exp_avg_sq, transition * transition, precision=lax.Precision.HIGHEST)
    grad_right = jnp.dot(grad, new_basis, preferred_element_type=jnp.float32).astype(jnp.bfloat16)
    grad_rotated = jnp.dot(left_basis.T, grad_right, preferred_element_type=jnp.float32)
    new_exp_avg = first_beta * first_moment + (1.0 - first_beta) * grad_rotated
    new_exp_avg_sq = second_beta * second_moment + (1.0 - second_beta) * grad_rotated * grad_rotated
    bias_first = 1.0 - first_beta ** STEP
    bias_second = 1.0 - second_beta ** STEP
    direction = (new_exp_avg / bias_first / (jnp.sqrt(new_exp_avg_sq / bias_second) + epsilon)).astype(jnp.bfloat16)
    partial_update = jnp.dot(left_basis, direction, preferred_element_type=jnp.float32).astype(jnp.bfloat16)
    update = jnp.dot(partial_update, new_basis.T, preferred_element_type=jnp.float32)
    return (new_exp_avg, new_exp_avg_sq, update)
```

```python
import jax
import jax.numpy as jnp
from jax import lax
from jax.experimental import pallas as pl
from jax.experimental.pallas import tpu as pltpu
from jax.sharding import PartitionSpec as P

STEP = 20
first_beta = 0.9
second_beta = 0.95
epsilon = 1e-08

N = 4096
FB = 256
RB = 512
NC = 4
CW = RB // NC
ROWS = 128
DEPTH = 3

BF = jnp.bfloat16
F32 = jnp.float32


def dot(a, b):
    return jnp.dot(a, b, preferred_element_type=F32)


class Wires:
    def __init__(self, send, recv):
        self.send, self.recv, self.count, self.out = send, recv, 0, []

    def copy(self, src, dst, device, landing):
        at = self.count
        self.count += 1

        def describe(a, b):
            return pltpu.make_async_remote_copy(
                src_ref=a,
                dst_ref=b,
                send_sem=self.send.at[at],
                recv_sem=self.recv.at[at],
                device_id=device,
                device_id_type=pl.DeviceIdType.MESH,
            )

        started = describe(src, dst)
        started.start()
        self.out.append(started)
        return describe(landing, landing).wait_recv

    def drain(self):
        for started in self.out:
            started.wait_send()


def kernel(
    grad, m1, m2, l_codes, l_scales, o_codes, o_scales, n_codes, n_scales,
    new_m1, new_m2, update,
    codes, o_slab, lb, nb, ob_t, tsend, town, trecv, tz_send, tz_recv, tf,
    mg, wcs, wcr, wown, wys, wyr, wsum, wzs, wzr, wb,
    gsend, gown, grecv, gz_send, gz_recv, mz_send, mz_recv, mown, df, pf,
    in_sem, o_sem, send_sem, recv_sem,
):
    f = lax.axis_index("fsdp")
    r = lax.axis_index("refresh")
    core, y, zh = lax.rem(f, 2), lax.rem(lax.div(f, 2), 4), lax.div(f, 8)
    x, zl = lax.rem(r, 4), lax.div(r, 4)

    def f_at(dz, dy, dc):
        zz = 1 - zh if dz else zh
        cc = 1 - core if dc else core
        return zz * 8 + lax.rem(y + dy + 4, 4) * 2 + cc

    def r_at(dz, dx):
        zz = 1 - zl if dz else zl
        return zz * 4 + lax.rem(x + dx + 4, 4)

    to_x = {d: (f, r_at(0, d)) for d in (1, 2, 3)}
    to_y = {d: (f_at(0, d, 0), r) for d in (1, 2, 3)}
    to_zl, to_zh, to_core = (f, r_at(1, 0)), (f_at(1, 0, 0), r), (f_at(0, 0, 1), r)
    wires = Wires(send_sem, recv_sem)

    jobs = [(n_codes, n_scales, nb, i) for i in range(2 * RB // (2 * ROWS))]
    jobs += [(l_codes, l_scales, lb, i) for i in range(FB // ROWS)]

    def fetch(job):
        src, _, _, i = jobs[job]
        return pltpu.make_async_copy(
            src.at[pl.ds(i * ROWS, ROWS), :], codes.at[job % DEPTH], in_sem.at[job % DEPTH]
        )

    o_in = [
        pltpu.make_async_copy(
            o_codes.at[:, pl.ds(pl.multiple_of(h * 2048 + f * 128, 128), 128)], o_slab.at[h], o_sem.at[h]
        )
        for h in range(2)
    ]
    for c in o_in:
        c.start()
    for job in range(DEPTH):
        fetch(job).start()

    barrier = pltpu.get_barrier_semaphore()
    friends = [*to_x.values(), *to_y.values(), to_zl, to_zh, to_core]
    for friend in friends:
        pl.semaphore_signal(barrier, inc=1, device_id=friend, device_id_type=pl.DeviceIdType.MESH)

    for h in range(2):
        o_in[h].wait()
        lanes = lax.broadcasted_iota(jnp.int32, (RB, 32), 1)
        scale = jnp.sum(jnp.where(lanes == f + 16 * h, o_scales[...], 0.0), axis=1, keepdims=True)
        values = (o_slab[h].astype(F32) - 7.5) * scale
        ob_t[pl.ds(h * 128, 128), :] = values.T.astype(BF)

    def expand(job):
        _, scales, out, i = jobs[job]
        fetch(job).wait()

        @pl.loop(0, ROWS // 32)
        def _(t):
            inner = pl.ds(pl.multiple_of(t * 32, 32), 32)
            outer = pl.ds(pl.multiple_of(i * ROWS + t * 32, 32), 32)
            s = scales[outer, :]
            for g in range(32):
                v = codes[job % DEPTH, inner, g * 128 : (g + 1) * 128].astype(F32) - 7.5
                out[outer, g * 128 : (g + 1) * 128] = (v * s[:, g : g + 1]).astype(BF)

        if job + DEPTH < len(jobs):
            fetch(job + DEPTH).start()

    for job in range(4):
        expand(job)

    for j in range(2):
        src = (m1, m2)[j]
        mg[pl.ds(x, 1), j] = src[...].astype(BF)[None]

    pl.semaphore_wait(barrier, len(friends))

    def columns(z, xx):
        return pl.ds(pl.multiple_of(z * 2048 + xx * RB, RB), RB)

    t_waits = []
    for d in (2, 1, 3):
        xx = lax.rem(x + d, 4)
        for z in range(2):
            tsend[d - 1, :, z * RB : (z + 1) * RB] = dot(ob_t[...], nb[:, columns(z, xx)]).astype(BF)
        t_waits.append(wires.copy(tsend.at[d - 1], trecv.at[d - 1], to_x[d], trecv.at[d - 1]))
    for z in range(2):
        town[:, z * RB : (z + 1) * RB] = dot(ob_t[...], nb[:, columns(z, x)])

    for job in range(4, len(jobs)):
        expand(job)

    def left_grad(block):
        lt = lb[:, pl.ds(pl.multiple_of(block * FB, FB), FB)]
        return lax.dot_general(lt, grad[...], (((0,), (0,)), ((), ())), preferred_element_type=F32)

    @pl.loop(0, 8)
    def _(q):
        wcs[q] = left_grad(lax.rem(q, 2) * 8 + lax.div(q, 2) * 2 + 1 - core).astype(BF)

    wc_wait = wires.copy(wcs, wcr, to_core, wcr)

    @pl.loop(0, 8)
    def _(q):
        wown[q] = left_grad(lax.rem(q, 2) * 8 + lax.div(q, 2) * 2 + core)

    wc_wait()
    wy_waits = []
    for d in (2, 1, 3):
        yy = lax.rem(y + d, 4)
        for z in range(2):
            wys[d - 1, z] = (wown[yy * 2 + z] + wcr[yy * 2 + z].astype(F32)).astype(BF)
        wy_waits.append(wires.copy(wys.at[d - 1], wyr.at[d - 1], to_y[d], wyr.at[d - 1]))
    for z in range(2):
        wsum[z] = wown[y * 2 + z] + wcr[y * 2 + z].astype(F32)

    for wait in t_waits:
        wait()
    m_waits = [
        wires.copy(mg.at[x], mg.at[x], to_x[d], mg.at[lax.rem(x + 4 - d, 4)]) for d in (2, 1, 3)
    ]

    def t_sum(z):
        rows = pl.ds(pl.multiple_of(z * 128, 128), 128)
        return (
            town[rows, :]
            + trecv[0, rows, :].astype(F32)
            + trecv[1, rows, :].astype(F32)
            + trecv[2, rows, :].astype(F32)
        )

    tz_send[...] = t_sum(1 - zl).astype(BF)
    tz_wait = wires.copy(tz_send, tz_recv, to_zl, tz_recv)
    tz_wait()
    tf[pl.ds(pl.multiple_of(f * 128, 128), 128), :] = (t_sum(zl) + tz_recv[...].astype(F32)).astype(BF)

    class Spread:
        def __init__(self, place):
            self.place = place
            own = place(f)
            self.a = {d: wires.copy(own, own, to_y[d], place(f_at(0, -d, 0))) for d in (2, 1, 3)}
            self.b = wires.copy(own, own, to_zh, place(f_at(1, 0, 0)))
            self.e = [wires.copy(own, own, to_core, place(f_at(0, 0, 1)))]

        def pass_core(self, dz, dy):
            block = self.place(f_at(dz, dy, 0))
            self.e.append(wires.copy(block, block, to_core, self.place(f_at(dz, dy, 1))))

        def pass_zh(self):
            self.b()
            block = self.place(f_at(1, 0, 0))
            self.c = {d: wires.copy(block, block, to_y[d], self.place(f_at(1, -d, 0))) for d in (2, 1, 3)}
            self.pass_core(1, 0)

        def pass_y(self):
            for d in (1, 3, 2):
                self.a[d]()
                self.pass_core(0, -d)
            for d in (1, 3, 2):
                self.c[d]()
                self.pass_core(1, -d)

        def finish(self):
            for wait in self.e:
                wait()

    spread_t = Spread(lambda i: tf.at[pl.ds(pl.multiple_of(i * 128, 128), 128), :])

    for wait in wy_waits:
        wait()

    def w_sum(z):
        return wsum[z] + wyr[0, z].astype(F32) + wyr[1, z].astype(F32) + wyr[2, z].astype(F32)

    wzs[...] = w_sum(1 - zh).astype(BF)
    wz_wait = wires.copy(wzs, wzr, to_zh, wzr)
    spread_t.pass_zh()
    wz_wait()
    wb[...] = (w_sum(zh) + wzr[...].astype(F32)).astype(BF)

    g_waits = []
    for d in (2, 1, 3):
        xx = lax.rem(x + d, 4)
        for z in range(2):
            gsend[d - 1, z] = dot(wb[...], nb[:, columns(z, xx)]).astype(BF)
        g_waits.append(wires.copy(gsend.at[d - 1], grecv.at[d - 1], to_x[d], grecv.at[d - 1]))
    for z in range(2):
        gown[z] = dot(wb[...], nb[:, columns(z, x)])

    spread_t.pass_y()
    spread_t.finish()
    for wait in m_waits:
        wait()

    half = 2 * CW

    def moments(z, c):
        cols = pl.ds(pl.multiple_of(z * RB + c * half, half), half)
        a = jnp.zeros((FB, half), F32)
        b = jnp.zeros((FB, half), F32)
        for k in range(4):
            t = tf[pl.ds(k * RB, RB), cols]
            a = a + dot(mg[k, 0], t)
            b = b + dot(mg[k, 1], t * t)
        return a, b

    mz_waits = []
    for c in range(2):
        a, b = moments(1 - zl, c)
        mz_send[c, 0] = a.astype(BF)
        mz_send[c, 1] = b.astype(BF)
        mz_waits.append(wires.copy(mz_send.at[c], mz_recv.at[c], to_zl, mz_recv.at[c]))

    for wait in g_waits:
        wait()

    def g_sum(z):
        return gown[z] + grecv[0, z].astype(F32) + grecv[1, z].astype(F32) + grecv[2, z].astype(F32)

    gz_send[...] = g_sum(1 - zl).astype(BF)
    gz_wait = wires.copy(gz_send, gz_recv, to_zl, gz_recv)
    for c in range(2):
        a, b = moments(zl, c)
        mown[c, 0] = a
        mown[c, 1] = b
    gz_wait()
    gown[pl.ds(zl, 1)] = (g_sum(zl) + gz_recv[...].astype(F32))[None]

    spreads = []
    for c in range(NC):
        h, off = (c * CW) // half, (c * CW) % half
        if off == 0:
            mz_waits[h]()
        cols = slice(c * CW, (c + 1) * CW)
        rot = gown[zl, :, cols]
        first = mown[h, 0, :, off : off + CW] + mz_recv[h, 0, :, off : off + CW].astype(F32)
        second = mown[h, 1, :, off : off + CW] + mz_recv[h, 1, :, off : off + CW].astype(F32)
        a = first_beta * first + (1.0 - first_beta) * rot
        b = second_beta * second + (1.0 - second_beta) * rot * rot
        new_m1[:, cols] = a
        new_m2[:, cols] = b
        bias_first = 1.0 - first_beta**STEP
        bias_second = 1.0 - second_beta**STEP
        direction = (a / bias_first) / (jnp.sqrt(b / bias_second) + epsilon)

        def place(i, c=c):
            return df.at[c, pl.ds(pl.multiple_of(i * FB, FB), FB), :]

        df[c, pl.ds(pl.multiple_of(f * FB, FB), FB), :] = direction.astype(BF)
        spreads.append(Spread(place))

    class Share:
        def __init__(self, place):
            self.place = place
            own = place(r)
            self.a = {d: wires.copy(own, own, to_x[d], place(r_at(0, -d))) for d in (2, 1, 3)}
            self.b = wires.copy(own, own, to_zl, place(r_at(1, 0)))

        def pass_zl(self):
            self.b()
            block = self.place(r_at(1, 0))
            self.c = {d: wires.copy(block, block, to_x[d], self.place(r_at(1, -d))) for d in (2, 1, 3)}

        def finish(self):
            for d in (1, 3, 2):
                self.a[d]()
            for d in (1, 3, 2):
                self.c[d]()

    shares = []
    for c in range(NC):
        spreads[c].pass_zh()
    for c in range(NC):
        spreads[c].pass_y()
        if c > 0:
            shares[c - 1].pass_zl()
        spreads[c].finish()
        pf[c, r] = dot(lb[...], df[c]).astype(BF)
        shares.append(Share(lambda i, c=c: pf.at[c, i]))
    shares[NC - 1].pass_zl()

    def update_part(c):
        total = jnp.zeros((FB, RB), F32)
        for i in range(8):
            n = nb[:, i * RB + c * CW : i * RB + (c + 1) * CW]
            total = total + lax.dot_general(pf[c, i], n, (((1,), (1,)), ((), ())), preferred_element_type=F32)
        return total

    for c in range(NC):
        shares[c].finish()
        if c == 0:
            update[...] = update_part(c)
        else:
            update[...] += update_part(c)
    wires.drain()


WIRES = 1 + 3 + 1 + 15 + 3 + 3 + 1 + 3 + 1 + 2 + NC * 22


def body(*args):
    vmem = pl.BlockSpec(memory_space=pltpu.VMEM)
    hbm = pl.BlockSpec(memory_space=pl.ANY)
    out = jax.ShapeDtypeStruct((FB, RB), F32)
    scratch = [
        pltpu.VMEM((DEPTH, ROWS, N), jnp.int32),
        pltpu.VMEM((2, RB, 128), jnp.int32),
        pltpu.VMEM((FB, N), BF),
        pltpu.VMEM((RB, N), BF),
        pltpu.VMEM((256, RB), BF),
        pltpu.VMEM((3, 256, 1024), BF),
        pltpu.VMEM((256, 1024), F32),
        pltpu.VMEM((3, 256, 1024), BF),
        pltpu.VMEM((128, 1024), BF),
        pltpu.VMEM((128, 1024), BF),
        pltpu.VMEM((2048, 1024), BF),
        pltpu.VMEM((4, 2, FB, RB), BF),
        pltpu.VMEM((8, FB, RB), BF),
        pltpu.VMEM((8, FB, RB), BF),
        pltpu.VMEM((8, FB, RB), F32),
        pltpu.VMEM((3, 2, FB, RB), BF),
        pltpu.VMEM((3, 2, FB, RB), BF),
        pltpu.VMEM((2, FB, RB), F32),
        pltpu.VMEM((FB, RB), BF),
        pltpu.VMEM((FB, RB), BF),
        pltpu.VMEM((FB, RB), BF),
        pltpu.VMEM((3, 2, FB, RB), BF),
        pltpu.VMEM((2, FB, RB), F32),
        pltpu.VMEM((3, 2, FB, RB), BF),
        pltpu.VMEM((FB, RB), BF),
        pltpu.VMEM((FB, RB), BF),
        pltpu.VMEM((2, 2, FB, RB // 2), BF),
        pltpu.VMEM((2, 2, FB, RB // 2), BF),
        pltpu.VMEM((2, 2, FB, RB // 2), F32),
        pltpu.VMEM((NC, N, CW), BF),
        pltpu.VMEM((NC, 8, FB, CW), BF),
        pltpu.SemaphoreType.DMA((DEPTH,)),
        pltpu.SemaphoreType.DMA((2,)),
        pltpu.SemaphoreType.DMA((WIRES,)),
        pltpu.SemaphoreType.DMA((WIRES,)),
    ]
    return pl.pallas_call(
        kernel,
        out_shape=(out, out, out),
        in_specs=[vmem, vmem, vmem, hbm, vmem, hbm, vmem, hbm, vmem],
        out_specs=(vmem, vmem, vmem),
        scratch_shapes=scratch,
        compiler_params=pltpu.CompilerParams(
            collective_id=0, has_side_effects=True, vmem_limit_bytes=62 * 2**20
        ),
    )(*args)


def solution(mesh):
    return jax.shard_map(
        body,
        mesh=mesh,
        in_specs=(
            P("fsdp", "refresh"),
            P("fsdp", "refresh"),
            P("fsdp", "refresh"),
            P("fsdp", None),
            P("fsdp", None),
            P("refresh", None),
            P("refresh", None),
            P("refresh", None),
            P("refresh", None),
        ),
        out_specs=(P("fsdp", "refresh"), P("fsdp", "refresh"), P("fsdp", "refresh")),
        check_vma=False,
    )
```

```python
import jax
import jax.numpy as jnp
from jax import lax
from jax.experimental import pallas as pl
from jax.experimental.pallas import tpu as pltpu
from jax.sharding import PartitionSpec as P

STEP = 20
first_beta = 0.9
second_beta = 0.95
epsilon = 1e-08

N = 4096
FB = 256
RB = 512
HB = RB // 2
NC = 4
CW = RB // NC
N_DEPTH, L_DEPTH = 6, 4

BF = jnp.bfloat16
F32 = jnp.float32


def dot(a, b):
    return jnp.dot(a, b, preferred_element_type=F32)


class Wires:
    def __init__(self, send, recv):
        self.send, self.recv, self.count, self.out = send, recv, 0, []

    def copy(self, src, dst, device, landing):
        at = self.count
        self.count += 1

        def describe(a, b):
            return pltpu.make_async_remote_copy(
                src_ref=a,
                dst_ref=b,
                send_sem=self.send.at[at],
                recv_sem=self.recv.at[at],
                device_id=device,
                device_id_type=pl.DeviceIdType.MESH,
            )

        started = describe(src, dst)
        started.start()
        self.out.append(started)
        return describe(landing, landing).wait_recv

    def drain(self):
        for started in self.out:
            started.wait_send()


class Ring:
    def __init__(self, wires, place, half, at, to):
        self.wires, self.place, self.half, self.at, self.to = wires, place, half, at, to
        own = place(at(0))
        self.up = wires.copy(own, own, to[1], place(at(-1)))
        self.down = wires.copy(own, own, to[3], place(at(1)))

    def forward(self):
        far = self.place(self.at(2))
        self.up()
        piece = self.half(self.place(self.at(-1)), 0)
        self.far_up = self.wires.copy(piece, piece, self.to[1], self.half(far, 0))
        self.down()
        piece = self.half(self.place(self.at(1)), 1)
        self.far_down = self.wires.copy(piece, piece, self.to[3], self.half(far, 1))

    def finish(self):
        self.far_up()
        self.far_down()


def kernel(
    grad, m1, m2, l_codes, l_scales, o_codes, o_scales, n_codes, n_scales,
    new_m1, new_m2, update,
    ncode, lcode, o_slab, lb, nb, n2, ob_t, tsend, town, trecv, tz_send, tz_recv, tf,
    mg, wcs, wcr, wys, wyr, wsum, wzs, wzr, wb, w2,
    gsend, gown, grecv, mz_send, mz_recv, mown, df, pf,
    n_sem, l_sem, o_sem, send_sem, recv_sem,
):
    f = lax.axis_index("fsdp")
    r = lax.axis_index("refresh")
    core, y, zh = lax.rem(f, 2), lax.rem(lax.div(f, 2), 4), lax.div(f, 8)
    x, zl = lax.rem(r, 4), lax.div(r, 4)

    def f_at(dz, dy, dc):
        zz = 1 - zh if dz else zh
        cc = 1 - core if dc else core
        return zz * 8 + lax.rem(y + dy + 4, 4) * 2 + cc

    def r_at(dz, dx):
        zz = 1 - zl if dz else zl
        return zz * 4 + lax.rem(x + dx + 4, 4)

    to_x = {d: (f, r_at(0, d)) for d in (1, 2, 3)}
    to_y = {d: (f_at(0, d, 0), r) for d in (1, 2, 3)}
    to_zl, to_zh, to_core = (f, r_at(1, 0)), (f_at(1, 0, 0), r), (f_at(0, 0, 1), r)
    wires = Wires(send_sem, recv_sem)

    def offset(v, unit):
        return pl.multiple_of(v, unit)

    n_jobs = [(z * 2048 + lax.rem(x + d, 4) * RB + h * HB) for h in range(2) for d in (2, 1, 3, 0) for z in range(2)]
    l_jobs = [(z * 2048 + lax.rem(y + d, 4) * RB) for d in (2, 1, 3, 0) for z in range(2)]

    def n_fetch(job):
        return pltpu.make_async_copy(
            n_codes.at[:, pl.ds(offset(n_jobs[job], HB), HB)], ncode.at[job % N_DEPTH], n_sem.at[job % N_DEPTH]
        )

    def l_fetch(job):
        return pltpu.make_async_copy(
            l_codes.at[:, pl.ds(offset(l_jobs[job], RB), RB)], lcode.at[job % L_DEPTH], l_sem.at[job % L_DEPTH]
        )

    o_in = [
        pltpu.make_async_copy(o_codes.at[:, pl.ds(offset(h * 2048 + f * 128, 128), 128)], o_slab.at[h], o_sem.at[h])
        for h in range(2)
    ]
    for c in o_in:
        c.start()
    for job in range(N_DEPTH):
        n_fetch(job).start()
    for job in range(L_DEPTH):
        l_fetch(job).start()

    barrier = pltpu.get_barrier_semaphore()
    friends = [*to_x.values(), *to_y.values(), to_zl, to_zh, to_core]
    for friend in friends:
        pl.semaphore_signal(barrier, inc=1, device_id=friend, device_id_type=pl.DeviceIdType.MESH)

    def widened(scales, group, rows):
        eight = scales[pl.ds(offset(lax.div(group, 8) * 8, 8), 8), rows * 128 : (rows + 1) * 128]
        chosen = lax.broadcasted_iota(jnp.int32, (8, 128), 0) == lax.rem(group, 8)
        row = jnp.sum(jnp.where(chosen, eight, 0.0), axis=0, keepdims=True)
        return jnp.broadcast_to(row, (128, 128)).T

    for h in range(2):
        o_in[h].wait()
        for b in range(4):
            values = (o_slab[h, b * 128 : (b + 1) * 128, :].astype(F32) - 7.5) * widened(o_scales, f + 16 * h, b)
            ob_t[h * 128 : (h + 1) * 128, b * 128 : (b + 1) * 128] = values.T.astype(BF)

    for j in range(2):
        mg[pl.ds(x, 1), j] = (m1, m2)[j][...].astype(BF)[None]

    def expand(slot, scales, out, column, rows, groups):
        for g in range(groups):
            for b in range(rows // 128):
                part = slice(b * 128, (b + 1) * 128)
                v = slot[part, g * 128 : (g + 1) * 128].astype(F32) - 7.5
                v = v * widened(scales, lax.div(column, 128) + g, b)
                out[part, pl.ds(offset(column + g * 128, 128), 128)] = v.astype(BF)

    def n_expand(job):
        n_fetch(job).wait()
        expand(ncode.at[job % N_DEPTH], n_scales, nb, n_jobs[job], RB, 2)
        if job + N_DEPTH < len(n_jobs):
            n_fetch(job + N_DEPTH).start()

    def l_expand(job):
        l_fetch(job).wait()
        expand(lcode.at[job % L_DEPTH], l_scales, lb, l_jobs[job], FB, 4)
        if job + L_DEPTH < len(l_jobs):
            l_fetch(job + L_DEPTH).start()

    t_waits = [[], []]
    for h in range(2):
        for i, d in enumerate((2, 1, 3, 0)):
            for z in range(2):
                job = (h * 4 + i) * 2 + z
                n_expand(job)
                part = dot(ob_t[...], nb[:, pl.ds(offset(n_jobs[job], HB), HB)])
                cols = slice(z * HB, (z + 1) * HB)
                if d:
                    tsend[h, d - 1, :, cols] = part.astype(BF)
                else:
                    town[h, :, cols] = part
            if h == 0 and i == 0:
                pl.semaphore_wait(barrier, len(friends))
            if d:
                t_waits[h].append(wires.copy(tsend.at[h, d - 1], trecv.at[h, d - 1], to_x[d], trecv.at[h, d - 1]))

    mine = pl.ds(offset(core * 256, 256), 256)
    theirs = pl.ds(offset((1 - core) * 256, 256), 256)
    n_wait = wires.copy(
        nb.at[mine, pl.ds(offset((1 - zl) * 2048, 2048), 2048)], n2.at[mine, :], to_zl, n2.at[mine, :]
    )

    def left_grad(z, d, c):
        lt = lb[:, pl.ds(offset(z * 2048 + lax.rem(y + d, 4) * RB + c * FB, FB), FB)]
        return lax.dot_general(lt, grad[...], (((0,), (0,)), ((), ())), preferred_element_type=F32)

    wc_waits, wy_waits = {}, []

    def send_w(d):
        parts = [left_grad(z, d, core) for z in range(2)]
        wc_waits[d]()
        for z in range(2):
            total = parts[z] + wcr[d, z].astype(F32)
            if d:
                wys[d - 1, z] = total.astype(BF)
            else:
                wsum[z] = total
        if d:
            wy_waits.append(wires.copy(wys.at[d - 1], wyr.at[d - 1], to_y[d], wyr.at[d - 1]))

    before = None
    for i, d in enumerate((2, 1, 3, 0)):
        for z in range(2):
            l_expand(2 * i + z)
            wcs[d, z] = left_grad(z, d, 1 - core).astype(BF)
        wc_waits[d] = wires.copy(wcs.at[d], wcr.at[d], to_core, wcr.at[d])
        if before is not None:
            send_w(before)
        before = d
    send_w(before)

    def t_sum(h, z):
        rows = pl.ds(offset(z * 128, 128), 128)
        total = town[h, rows, :]
        for k in range(3):
            total = total + trecv[h, k, rows, :].astype(F32)
        return total

    def t_swap(h):
        for wait in t_waits[h]:
            wait()
        tz_send[h] = t_sum(h, 1 - zl).astype(BF)
        return wires.copy(tz_send.at[h], tz_recv.at[h], to_zl, tz_recv.at[h])

    def t_place(h):
        return lambda i: tf.at[h, pl.ds(offset(i * 128, 128), 128), :]

    def t_own(h):
        tf[h, pl.ds(offset(f * 128, 128), 128), :] = (t_sum(h, zl) + tz_recv[h].astype(F32)).astype(BF)

    def half_of(rows):
        return lambda block, k: block.at[pl.ds(k * rows, rows), :]

    class Spread:
        def __init__(self, place, rows):
            self.place, self.half = place, half_of(rows // 2)
            own = place(f)
            self.z = wires.copy(own, own, to_zh, place(f_at(1, 0, 0)))
            self.e = [wires.copy(own, own, to_core, place(f_at(0, 0, 1)))]

        def pass_core(self, dz, dy):
            block = self.place(f_at(dz, dy, 0))
            self.e.append(wires.copy(block, block, to_core, self.place(f_at(dz, dy, 1))))

        def start(self):
            self.near = Ring(wires, self.place, self.half, lambda d: f_at(0, d, 0), to_y)
            self.z()
            self.other = Ring(wires, self.place, self.half, lambda d: f_at(1, d, 0), to_y)
            self.pass_core(1, 0)

        def forward(self):
            for dz, ring in enumerate((self.near, self.other)):
                ring.forward()
                self.pass_core(dz, 1)
                self.pass_core(dz, -1)

        def finish(self):
            for dz, ring in enumerate((self.near, self.other)):
                ring.finish()
                self.pass_core(dz, 2)
            for wait in self.e:
                wait()

    tz_wait = t_swap(0)
    tz_wait()
    t_own(0)
    spread_t = [Spread(t_place(0), 128)]
    spread_t[0].start()
    tz_wait = t_swap(1)
    ring_m = Ring(wires, lambda i: mg.at[i], lambda block, k: block.at[k], lambda d: lax.rem(x + d + 4, 4), to_x)
    n_wait()
    n_core_wait = wires.copy(n2.at[mine, :], n2.at[mine, :], to_core, n2.at[theirs, :])
    tz_wait()
    t_own(1)
    spread_t.append(Spread(t_place(1), 128))
    spread_t[0].forward()

    for wait in wy_waits:
        wait()

    def w_sum(z):
        total = wsum[z]
        for k in range(3):
            total = total + wyr[k, z].astype(F32)
        return total

    wzs[...] = w_sum(1 - zh).astype(BF)
    wz_wait = wires.copy(wzs, wzr, to_zh, wzr)
    spread_t[1].start()
    wz_wait()
    wb[...] = (w_sum(zh) + wzr[...].astype(F32)).astype(BF)
    w2_wait = wires.copy(wb, w2, to_zl, w2)
    ring_m.forward()
    spread_t[0].finish()
    w2_wait()
    n_core_wait()

    def rotated(d):
        xx = lax.rem(x + d, 4)
        here = dot(wb[...], nb[:, pl.ds(offset(zl * 2048 + xx * RB, RB), RB)])
        return here + dot(w2[...], n2[:, pl.ds(offset(xx * RB, RB), RB)])

    g_waits = []
    for d in (2, 1, 3):
        gsend[d - 1] = rotated(d).astype(BF)
        g_waits.append(wires.copy(gsend.at[d - 1], grecv.at[d - 1], to_x[d], grecv.at[d - 1]))
    gown[...] = rotated(0)

    def moments(z, h):
        a = jnp.zeros((FB, HB), F32)
        b = jnp.zeros((FB, HB), F32)
        for k in range(4):
            t = tf[h, pl.ds(k * RB, RB), pl.ds(offset(z * HB, HB), HB)]
            a = a + dot(mg[k, 0], t)
            b = b + dot(mg[k, 1], t * t)
        return a, b

    def m_swap(h):
        a, b = moments(1 - zl, h)
        mz_send[h, 0] = a.astype(BF)
        mz_send[h, 1] = b.astype(BF)
        return wires.copy(mz_send.at[h], mz_recv.at[h], to_zl, mz_recv.at[h])

    spread_t[1].forward()
    ring_m.finish()
    mz_waits = [m_swap(0)]
    mown[0, 0], mown[0, 1] = moments(zl, 0)
    spread_t[1].finish()
    mz_waits.append(m_swap(1))
    mown[1, 0], mown[1, 1] = moments(zl, 1)
    for wait in g_waits:
        wait()

    spreads = []
    for c in range(NC):
        h, off = (c * CW) // HB, (c * CW) % HB
        if off == 0:
            mz_waits[h]()
        cols = slice(c * CW, (c + 1) * CW)
        rot = gown[:, cols]
        for k in range(3):
            rot = rot + grecv[k, :, cols].astype(F32)
        first = mown[h, 0, :, off : off + CW] + mz_recv[h, 0, :, off : off + CW].astype(F32)
        second = mown[h, 1, :, off : off + CW] + mz_recv[h, 1, :, off : off + CW].astype(F32)
        a = first_beta * first + (1.0 - first_beta) * rot
        b = second_beta * second + (1.0 - second_beta) * rot * rot
        new_m1[:, cols] = a
        new_m2[:, cols] = b
        bias_first = 1.0 - first_beta**STEP
        bias_second = 1.0 - second_beta**STEP
        direction = (a / bias_first) / (jnp.sqrt(b / bias_second) + epsilon)

        def place(i, c=c):
            return df.at[c, pl.ds(offset(i * FB, FB), FB), :]

        df[c, pl.ds(offset(f * FB, FB), FB), :] = direction.astype(BF)
        spreads.append(Spread(place, FB))

    class Share:
        def __init__(self, place):
            self.place = place
            own = place(r)
            self.z = wires.copy(own, own, to_zl, place(r_at(1, 0)))
            self.near = Ring(wires, place, half_of(FB // 2), lambda d: r_at(0, d), to_x)

        def start(self):
            self.z()
            self.other = Ring(wires, self.place, half_of(FB // 2), lambda d: r_at(1, d), to_x)

        def forward(self):
            self.near.forward()
            self.other.forward()

        def finish(self):
            self.near.finish()
            self.other.finish()

    def update_part(c):
        total = jnp.zeros((FB, RB), F32)
        for i in range(8):
            n = nb[:, i * RB + c * CW : i * RB + (c + 1) * CW]
            total = total + lax.dot_general(pf[c, i], n, (((1,), (1,)), ((), ())), preferred_element_type=F32)
        if c == 0:
            update[...] = total
        else:
            update[...] += total

    shares = []
    spreads[0].start()
    for c in range(NC):
        if c + 1 < NC:
            spreads[c + 1].start()
        spreads[c].forward()
        if c >= 1:
            shares[c - 1].start()
        spreads[c].finish()
        pf[c, r] = dot(lb[...], df[c]).astype(BF)
        shares.append(Share(lambda i, c=c: pf.at[c, i]))
        if c >= 1:
            shares[c - 1].forward()
        if c >= 2:
            shares[c - 2].finish()
            update_part(c - 2)
    shares[NC - 1].start()
    shares[NC - 2].finish()
    update_part(NC - 2)
    shares[NC - 1].forward()
    shares[NC - 1].finish()
    update_part(NC - 1)
    wires.drain()


WIRES = 6 + 2 + 4 + 3 + 2 + 2 + 2 * 17 + 4 + 3 + 2 + NC * (17 + 9)


def hand_over(*refs):
    for given, result in zip(refs[:3], refs[3:]):
        result[...] = given[...]


def body(
    grad, exp_avg, exp_avg_sq, left_codes, left_scales,
    right_old_codes, right_old_scales, right_new_codes, right_new_scales,
):
    vmem = pl.BlockSpec(memory_space=pltpu.VMEM)
    hbm = pl.BlockSpec(memory_space=pl.ANY)
    out = jax.ShapeDtypeStruct((FB, RB), F32)
    scratch = [
        pltpu.VMEM((N_DEPTH, RB, HB), jnp.int32),
        pltpu.VMEM((L_DEPTH, FB, RB), jnp.int32),
        pltpu.VMEM((2, RB, 128), jnp.int32),
        pltpu.VMEM((FB, N), BF),
        pltpu.VMEM((RB, N), BF),
        pltpu.VMEM((RB, N // 2), BF),
        pltpu.VMEM((256, RB), BF),
        pltpu.VMEM((2, 3, 256, RB), BF),
        pltpu.VMEM((2, 256, RB), F32),
        pltpu.VMEM((2, 3, 256, RB), BF),
        pltpu.VMEM((2, 128, RB), BF),
        pltpu.VMEM((2, 128, RB), BF),
        pltpu.VMEM((2, N // 2, RB), BF),
        pltpu.VMEM((4, 2, FB, RB), BF),
        pltpu.VMEM((4, 2, FB, RB), BF),
        pltpu.VMEM((4, 2, FB, RB), BF),
        pltpu.VMEM((3, 2, FB, RB), BF),
        pltpu.VMEM((3, 2, FB, RB), BF),
        pltpu.VMEM((2, FB, RB), F32),
        pltpu.VMEM((FB, RB), BF),
        pltpu.VMEM((FB, RB), BF),
        pltpu.VMEM((FB, RB), BF),
        pltpu.VMEM((FB, RB), BF),
        pltpu.VMEM((3, FB, RB), BF),
        pltpu.VMEM((FB, RB), F32),
        pltpu.VMEM((3, FB, RB), BF),
        pltpu.VMEM((2, 2, FB, HB), BF),
        pltpu.VMEM((2, 2, FB, HB), BF),
        pltpu.VMEM((2, 2, FB, HB), F32),
        pltpu.VMEM((NC, N, CW), BF),
        pltpu.VMEM((NC, 8, FB, CW), BF),
        pltpu.SemaphoreType.DMA((N_DEPTH,)),
        pltpu.SemaphoreType.DMA((L_DEPTH,)),
        pltpu.SemaphoreType.DMA((2,)),
        pltpu.SemaphoreType.DMA((WIRES,)),
        pltpu.SemaphoreType.DMA((WIRES,)),
    ]
    results = pl.pallas_call(
        kernel,
        out_shape=(out, out, out),
        in_specs=[vmem, vmem, vmem, hbm, vmem, hbm, vmem, hbm, vmem],
        out_specs=(vmem, vmem, vmem),
        scratch_shapes=scratch,
        compiler_params=pltpu.CompilerParams(
            collective_id=0, has_side_effects=True, vmem_limit_bytes=62 * 2**20
        ),
    )(
        grad, exp_avg, exp_avg_sq, left_codes, left_scales.T,
        right_old_codes, right_old_scales.T, right_new_codes, right_new_scales.T,
    )
    return pl.pallas_call(
        hand_over,
        out_shape=(out, out, out),
        in_specs=[vmem] * 3,
        out_specs=(vmem,) * 3,
    )(*results)


def solution(mesh):
    return jax.shard_map(
        body,
        mesh=mesh,
        in_specs=(
            P("fsdp", "refresh"),
            P("fsdp", "refresh"),
            P("fsdp", "refresh"),
            P("fsdp", None),
            P("fsdp", None),
            P("refresh", None),
            P("refresh", None),
            P("refresh", None),
            P("refresh", None),
        ),
        out_specs=(P("fsdp", "refresh"), P("fsdp", "refresh"), P("fsdp", "refresh")),
        check_vma=False,
    )
```

```python
import jax
import jax.numpy as jnp
from jax import lax
from jax.experimental import pallas as pl
from jax.experimental.pallas import tpu as pltpu
from jax.sharding import PartitionSpec as P

STEP = 20
first_beta = 0.9
second_beta = 0.95
epsilon = 1e-08

N = 4096
FB = 256
RB = 512
HB = RB // 2
NC = 4
CW = RB // NC
N_DEPTH, L_DEPTH = 6, 4

BF = jnp.bfloat16
F32 = jnp.float32


def dot(a, b):
    return jnp.dot(a, b, preferred_element_type=F32)


class Wires:
    def __init__(self, send, recv):
        self.send, self.recv, self.count, self.out = send, recv, 0, []

    def copy(self, src, dst, device, landing):
        at = self.count
        self.count += 1

        def describe(a, b):
            return pltpu.make_async_remote_copy(
                src_ref=a,
                dst_ref=b,
                send_sem=self.send.at[at],
                recv_sem=self.recv.at[at],
                device_id=device,
                device_id_type=pl.DeviceIdType.MESH,
            )

        started = describe(src, dst)
        started.start()
        self.out.append(started)
        return describe(landing, landing).wait_recv

    def drain(self):
        for started in self.out:
            started.wait_send()


class Ring:
    def __init__(self, wires, place, half, at, to):
        self.wires, self.place, self.half, self.at, self.to = wires, place, half, at, to
        own = place(at(0))
        self.up = wires.copy(own, own, to[1], place(at(-1)))
        self.down = wires.copy(own, own, to[3], place(at(1)))

    def forward(self):
        far = self.place(self.at(2))
        self.up()
        piece = self.half(self.place(self.at(-1)), 0)
        self.far_up = self.wires.copy(piece, piece, self.to[1], self.half(far, 0))
        self.down()
        piece = self.half(self.place(self.at(1)), 1)
        self.far_down = self.wires.copy(piece, piece, self.to[3], self.half(far, 1))

    def finish(self):
        self.far_up()
        self.far_down()


def kernel(
    grad, m1, m2, l_codes, l_scales, o_codes, o_scales, n_codes, n_scales,
    new_m1, new_m2, update,
    ncode, lcode, o_slab, lb, nb, n2, ob_t, tsend, town, trecv, tz_send, tz_recv, tf,
    mg, wcs, wcr, wys, wyr, wsum, wzs, wzr, wb, w2,
    gsend, gown, grecv, mz_send, mz_recv, mown, df, pf,
    n_sem, l_sem, o_sem, send_sem, recv_sem,
):
    f = lax.axis_index("fsdp")
    r = lax.axis_index("refresh")
    core, y, zh = lax.rem(f, 2), lax.rem(lax.div(f, 2), 4), lax.div(f, 8)
    x, zl = lax.rem(r, 4), lax.div(r, 4)

    def f_at(dz, dy, dc):
        zz = 1 - zh if dz else zh
        cc = 1 - core if dc else core
        return zz * 8 + lax.rem(y + dy + 4, 4) * 2 + cc

    def r_at(dz, dx):
        zz = 1 - zl if dz else zl
        return zz * 4 + lax.rem(x + dx + 4, 4)

    to_x = {d: (f, r_at(0, d)) for d in (1, 2, 3)}
    to_y = {d: (f_at(0, d, 0), r) for d in (1, 2, 3)}
    to_zl, to_zh, to_core = (f, r_at(1, 0)), (f_at(1, 0, 0), r), (f_at(0, 0, 1), r)
    wires = Wires(send_sem, recv_sem)

    def offset(v, unit):
        return pl.multiple_of(v, unit)

    n_jobs = [(z * 2048 + lax.rem(x + d, 4) * RB + h * HB) for h in range(2) for d in (2, 1, 3, 0) for z in range(2)]
    l_jobs = [(z * 2048 + lax.rem(y + d, 4) * RB) for d in (2, 1, 3, 0) for z in range(2)]

    def n_fetch(job):
        return pltpu.make_async_copy(
            n_codes.at[:, pl.ds(offset(n_jobs[job], HB), HB)], ncode.at[job % N_DEPTH], n_sem.at[job % N_DEPTH]
        )

    def l_fetch(job):
        return pltpu.make_async_copy(
            l_codes.at[:, pl.ds(offset(l_jobs[job], RB), RB)], lcode.at[job % L_DEPTH], l_sem.at[job % L_DEPTH]
        )

    o_in = [
        pltpu.make_async_copy(o_codes.at[:, pl.ds(offset(h * 2048 + f * 128, 128), 128)], o_slab.at[h], o_sem.at[h])
        for h in range(2)
    ]
    for c in o_in:
        c.start()
    for job in range(N_DEPTH):
        n_fetch(job).start()
    for job in range(L_DEPTH):
        l_fetch(job).start()

    barrier = pltpu.get_barrier_semaphore()
    friends = [*to_x.values(), *to_y.values(), to_zl, to_zh, to_core]
    for friend in friends:
        pl.semaphore_signal(barrier, inc=1, device_id=friend, device_id_type=pl.DeviceIdType.MESH)

    def widened(scales, group, rows):
        eight = scales[pl.ds(offset(lax.div(group, 8) * 8, 8), 8), rows * 128 : (rows + 1) * 128]
        chosen = lax.broadcasted_iota(jnp.int32, (8, 128), 0) == lax.rem(group, 8)
        row = jnp.sum(jnp.where(chosen, eight, 0.0), axis=0, keepdims=True)
        return jnp.broadcast_to(row, (128, 128)).T

    for h in range(2):
        o_in[h].wait()
        for b in range(4):
            values = (o_slab[h, b * 128 : (b + 1) * 128, :].astype(F32) - 7.5) * widened(o_scales, f + 16 * h, b)
            ob_t[h * 128 : (h + 1) * 128, b * 128 : (b + 1) * 128] = values.T.astype(BF)

    for j in range(2):
        mg[pl.ds(x, 1), j] = (m1, m2)[j][...].astype(BF)[None]

    def expand(slot, scales, out, column, rows, groups):
        for g in range(groups):
            for b in range(rows // 128):
                part = slice(b * 128, (b + 1) * 128)
                v = slot[part, g * 128 : (g + 1) * 128].astype(F32) - 7.5
                v = v * widened(scales, lax.div(column, 128) + g, b)
                out[part, pl.ds(offset(column + g * 128, 128), 128)] = v.astype(BF)

    def n_expand(job):
        n_fetch(job).wait()
        expand(ncode.at[job % N_DEPTH], n_scales, nb, n_jobs[job], RB, 2)
        if job + N_DEPTH < len(n_jobs):
            n_fetch(job + N_DEPTH).start()

    def l_expand(job):
        l_fetch(job).wait()
        expand(lcode.at[job % L_DEPTH], l_scales, lb, l_jobs[job], FB, 4)
        if job + L_DEPTH < len(l_jobs):
            l_fetch(job + L_DEPTH).start()

    mine = pl.ds(offset(core * 256, 256), 256)
    theirs = pl.ds(offset((1 - core) * 256, 256), 256)
    n_waits = []

    def n_swap(h, d):
        within = lax.rem(x + d, 4) * RB + h * HB
        landing = n2.at[mine, pl.ds(offset(within, HB), HB)]
        src = nb.at[mine, pl.ds(offset((1 - zl) * 2048 + within, HB), HB)]
        n_waits.append(wires.copy(src, landing, to_zl, landing))

    t_waits = [[], []]

    def t_part(h):
        for i, d in enumerate((2, 1, 3, 0)):
            for z in range(2):
                job = (h * 4 + i) * 2 + z
                n_expand(job)
                part = dot(ob_t[...], nb[:, pl.ds(offset(n_jobs[job], HB), HB)])
                cols = slice(z * HB, (z + 1) * HB)
                if d:
                    tsend[h, d - 1, :, cols] = part.astype(BF)
                else:
                    town[h, :, cols] = part
            if h == 0 and i == 0:
                pl.semaphore_wait(barrier, len(friends))
            if d:
                t_waits[h].append(wires.copy(tsend.at[h, d - 1], trecv.at[h, d - 1], to_x[d], trecv.at[h, d - 1]))
            n_swap(h, d)

    t_part(0)

    def left_grad(z, d, c):
        lt = lb[:, pl.ds(offset(z * 2048 + lax.rem(y + d, 4) * RB + c * FB, FB), FB)]
        return lax.dot_general(lt, grad[...], (((0,), (0,)), ((), ())), preferred_element_type=F32)

    wc_waits, wy_waits = {}, []

    def send_w(d):
        parts = [left_grad(z, d, core) for z in range(2)]
        wc_waits[d]()
        for z in range(2):
            total = parts[z] + wcr[d, z].astype(F32)
            if d:
                wys[d - 1, z] = total.astype(BF)
            else:
                wsum[z] = total
        if d:
            wy_waits.append(wires.copy(wys.at[d - 1], wyr.at[d - 1], to_y[d], wyr.at[d - 1]))

    before = None
    for i, d in enumerate((2, 1, 3, 0)):
        for z in range(2):
            l_expand(2 * i + z)
            wcs[d, z] = left_grad(z, d, 1 - core).astype(BF)
        wc_waits[d] = wires.copy(wcs.at[d], wcr.at[d], to_core, wcr.at[d])
        if before is not None:
            send_w(before)
        before = d
    send_w(before)

    t_part(1)


    def t_sum(h, z):
        rows = pl.ds(offset(z * 128, 128), 128)
        total = town[h, rows, :]
        for k in range(3):
            total = total + trecv[h, k, rows, :].astype(F32)
        return total

    def t_swap(h):
        for wait in t_waits[h]:
            wait()
        tz_send[h] = t_sum(h, 1 - zl).astype(BF)
        return wires.copy(tz_send.at[h], tz_recv.at[h], to_zl, tz_recv.at[h])

    def t_place(h):
        return lambda i: tf.at[h, pl.ds(offset(i * 128, 128), 128), :]

    def t_own(h):
        tf[h, pl.ds(offset(f * 128, 128), 128), :] = (t_sum(h, zl) + tz_recv[h].astype(F32)).astype(BF)

    def half_of(rows):
        return lambda block, k: block.at[pl.ds(k * rows, rows), :]

    class Spread:
        def __init__(self, place, rows):
            self.place, self.half = place, half_of(rows // 2)
            own = place(f)
            self.z = wires.copy(own, own, to_zh, place(f_at(1, 0, 0)))
            self.e = [wires.copy(own, own, to_core, place(f_at(0, 0, 1)))]

        def pass_core(self, dz, dy):
            block = self.place(f_at(dz, dy, 0))
            self.e.append(wires.copy(block, block, to_core, self.place(f_at(dz, dy, 1))))

        def start(self):
            self.near = Ring(wires, self.place, self.half, lambda d: f_at(0, d, 0), to_y)
            self.z()
            self.other = Ring(wires, self.place, self.half, lambda d: f_at(1, d, 0), to_y)
            self.pass_core(1, 0)

        def forward(self):
            for dz, ring in enumerate((self.near, self.other)):
                ring.forward()
                self.pass_core(dz, 1)
                self.pass_core(dz, -1)

        def finish(self):
            for dz, ring in enumerate((self.near, self.other)):
                ring.finish()
                self.pass_core(dz, 2)
            for wait in self.e:
                wait()

    tz_wait = t_swap(0)
    tz_wait()
    t_own(0)
    spread_t = [Spread(t_place(0), 128)]
    spread_t[0].start()
    tz_wait = t_swap(1)
    ring_m = Ring(wires, lambda i: mg.at[i], lambda block, k: block.at[k], lambda d: lax.rem(x + d + 4, 4), to_x)

    def w_sum(z):
        total = wsum[z]
        for k in range(3):
            total = total + wyr[k, z].astype(F32)
        return total

    for wait in wy_waits:
        wait()
    wzs[...] = w_sum(1 - zh).astype(BF)
    wz_wait = wires.copy(wzs, wzr, to_zh, wzr)
    tz_wait()
    t_own(1)
    spread_t.append(Spread(t_place(1), 128))
    spread_t[0].forward()
    wz_wait()
    wb[...] = (w_sum(zh) + wzr[...].astype(F32)).astype(BF)
    w2_wait = wires.copy(wb, w2, to_zl, w2)
    spread_t[1].start()
    for wait in n_waits:
        wait()
    n_core_wait = wires.copy(n2.at[mine, :], n2.at[mine, :], to_core, n2.at[theirs, :])
    spread_t[0].finish()
    ring_m.forward()
    w2_wait()
    n_core_wait()

    def rotated(d):
        xx = lax.rem(x + d, 4)
        here = dot(wb[...], nb[:, pl.ds(offset(zl * 2048 + xx * RB, RB), RB)])
        return here + dot(w2[...], n2[:, pl.ds(offset(xx * RB, RB), RB)])

    g_waits = []
    for d in (2, 1, 3):
        gsend[d - 1] = rotated(d).astype(BF)
        g_waits.append(wires.copy(gsend.at[d - 1], grecv.at[d - 1], to_x[d], grecv.at[d - 1]))
    gown[...] = rotated(0)

    def moments(z, h):
        a = jnp.zeros((FB, HB), F32)
        b = jnp.zeros((FB, HB), F32)
        for k in range(4):
            t = tf[h, pl.ds(k * RB, RB), pl.ds(offset(z * HB, HB), HB)]
            a = a + dot(mg[k, 0], t)
            b = b + dot(mg[k, 1], t * t)
        return a, b

    def m_swap(h):
        a, b = moments(1 - zl, h)
        mz_send[h, 0] = a.astype(BF)
        mz_send[h, 1] = b.astype(BF)
        return wires.copy(mz_send.at[h], mz_recv.at[h], to_zl, mz_recv.at[h])

    spread_t[1].forward()
    ring_m.finish()
    mz_waits = [m_swap(0)]
    mown[0, 0], mown[0, 1] = moments(zl, 0)
    spread_t[1].finish()
    mz_waits.append(m_swap(1))
    mown[1, 0], mown[1, 1] = moments(zl, 1)
    for wait in g_waits:
        wait()

    spreads = []
    for c in range(NC):
        h, off = (c * CW) // HB, (c * CW) % HB
        if off == 0:
            mz_waits[h]()
        cols = slice(c * CW, (c + 1) * CW)
        rot = gown[:, cols]
        for k in range(3):
            rot = rot + grecv[k, :, cols].astype(F32)
        first = mown[h, 0, :, off : off + CW] + mz_recv[h, 0, :, off : off + CW].astype(F32)
        second = mown[h, 1, :, off : off + CW] + mz_recv[h, 1, :, off : off + CW].astype(F32)
        a = first_beta * first + (1.0 - first_beta) * rot
        b = second_beta * second + (1.0 - second_beta) * rot * rot
        new_m1[:, cols] = a
        new_m2[:, cols] = b
        bias_first = 1.0 - first_beta**STEP
        bias_second = 1.0 - second_beta**STEP
        direction = (a / bias_first) / (jnp.sqrt(b / bias_second) + epsilon)

        def place(i, c=c):
            return df.at[c, pl.ds(offset(i * FB, FB), FB), :]

        df[c, pl.ds(offset(f * FB, FB), FB), :] = direction.astype(BF)
        spreads.append(Spread(place, FB))

    class Share:
        def __init__(self, place):
            self.place = place
            own = place(r)
            self.z = wires.copy(own, own, to_zl, place(r_at(1, 0)))
            self.near = Ring(wires, place, half_of(FB // 2), lambda d: r_at(0, d), to_x)

        def start(self):
            self.z()
            self.other = Ring(wires, self.place, half_of(FB // 2), lambda d: r_at(1, d), to_x)

        def forward(self):
            self.near.forward()
            self.other.forward()

        def finish(self):
            self.near.finish()
            self.other.finish()

    def update_part(c):
        total = jnp.zeros((FB, RB), F32)
        for i in range(8):
            n = nb[:, i * RB + c * CW : i * RB + (c + 1) * CW]
            total = total + lax.dot_general(pf[c, i], n, (((1,), (1,)), ((), ())), preferred_element_type=F32)
        if c == 0:
            update[...] = total
        else:
            update[...] += total

    shares = []
    spreads[0].start()
    spreads[1].start()
    spreads[0].forward()
    for c in range(NC):
        if c + 2 < NC:
            spreads[c + 2].start()
        if c + 1 < NC:
            spreads[c + 1].forward()
        if c >= 1:
            shares[c - 1].start()
        spreads[c].finish()
        pf[c, r] = dot(lb[...], df[c]).astype(BF)
        shares.append(Share(lambda i, c=c: pf.at[c, i]))
        if c >= 1:
            shares[c - 1].forward()
        if c >= 2:
            shares[c - 2].finish()
            update_part(c - 2)
    shares[NC - 1].start()
    shares[NC - 2].finish()
    update_part(NC - 2)
    shares[NC - 1].forward()
    shares[NC - 1].finish()
    update_part(NC - 1)
    wires.drain()


WIRES = 6 + 9 + 4 + 3 + 2 + 2 + 2 * 17 + 4 + 3 + 2 + NC * (17 + 9)


def hand_over(*refs):
    for given, result in zip(refs[:3], refs[3:]):
        result[...] = given[...]


def body(
    grad, exp_avg, exp_avg_sq, left_codes, left_scales,
    right_old_codes, right_old_scales, right_new_codes, right_new_scales,
):
    vmem = pl.BlockSpec(memory_space=pltpu.VMEM)
    hbm = pl.BlockSpec(memory_space=pl.ANY)
    out = jax.ShapeDtypeStruct((FB, RB), F32)
    scratch = [
        pltpu.VMEM((N_DEPTH, RB, HB), jnp.int32),
        pltpu.VMEM((L_DEPTH, FB, RB), jnp.int32),
        pltpu.VMEM((2, RB, 128), jnp.int32),
        pltpu.VMEM((FB, N), BF),
        pltpu.VMEM((RB, N), BF),
        pltpu.VMEM((RB, N // 2), BF),
        pltpu.VMEM((256, RB), BF),
        pltpu.VMEM((2, 3, 256, RB), BF),
        pltpu.VMEM((2, 256, RB), F32),
        pltpu.VMEM((2, 3, 256, RB), BF),
        pltpu.VMEM((2, 128, RB), BF),
        pltpu.VMEM((2, 128, RB), BF),
        pltpu.VMEM((2, N // 2, RB), BF),
        pltpu.VMEM((4, 2, FB, RB), BF),
        pltpu.VMEM((4, 2, FB, RB), BF),
        pltpu.VMEM((4, 2, FB, RB), BF),
        pltpu.VMEM((3, 2, FB, RB), BF),
        pltpu.VMEM((3, 2, FB, RB), BF),
        pltpu.VMEM((2, FB, RB), F32),
        pltpu.VMEM((FB, RB), BF),
        pltpu.VMEM((FB, RB), BF),
        pltpu.VMEM((FB, RB), BF),
        pltpu.VMEM((FB, RB), BF),
        pltpu.VMEM((3, FB, RB), BF),
        pltpu.VMEM((FB, RB), F32),
        pltpu.VMEM((3, FB, RB), BF),
        pltpu.VMEM((2, 2, FB, HB), BF),
        pltpu.VMEM((2, 2, FB, HB), BF),
        pltpu.VMEM((2, 2, FB, HB), F32),
        pltpu.VMEM((NC, N, CW), BF),
        pltpu.VMEM((NC, 8, FB, CW), BF),
        pltpu.SemaphoreType.DMA((N_DEPTH,)),
        pltpu.SemaphoreType.DMA((L_DEPTH,)),
        pltpu.SemaphoreType.DMA((2,)),
        pltpu.SemaphoreType.DMA((WIRES,)),
        pltpu.SemaphoreType.DMA((WIRES,)),
    ]
    results = pl.pallas_call(
        kernel,
        out_shape=(out, out, out),
        in_specs=[vmem, vmem, vmem, hbm, vmem, hbm, vmem, hbm, vmem],
        out_specs=(vmem, vmem, vmem),
        scratch_shapes=scratch,
        compiler_params=pltpu.CompilerParams(
            collective_id=0, has_side_effects=True, vmem_limit_bytes=62 * 2**20
        ),
    )(
        grad, exp_avg, exp_avg_sq, left_codes, left_scales.T,
        right_old_codes, right_old_scales.T, right_new_codes, right_new_scales.T,
    )
    return pl.pallas_call(
        hand_over,
        out_shape=(out, out, out),
        in_specs=[vmem] * 3,
        out_specs=(vmem,) * 3,
    )(*results)


def solution(mesh):
    return jax.shard_map(
        body,
        mesh=mesh,
        in_specs=(
            P("fsdp", "refresh"),
            P("fsdp", "refresh"),
            P("fsdp", "refresh"),
            P("fsdp", None),
            P("fsdp", None),
            P("refresh", None),
            P("refresh", None),
            P("refresh", None),
            P("refresh", None),
        ),
        out_specs=(P("fsdp", "refresh"), P("fsdp", "refresh"), P("fsdp", "refresh")),
        check_vma=False,
    )
```

```python
import jax
import jax.numpy as jnp
from jax import lax
from jax.experimental import pallas as pl
from jax.experimental.pallas import tpu as pltpu
from jax.sharding import PartitionSpec as P

STEP = 20
first_beta = 0.9
second_beta = 0.95
epsilon = 1e-08

N = 4096
FB = 256
RB = 512
HB = RB // 2
NC = 4
CW = RB // NC
N_DEPTH, L_DEPTH = 6, 4

BF = jnp.bfloat16
F32 = jnp.float32


def dot(a, b):
    return jnp.dot(a, b, preferred_element_type=F32)


class Wires:
    def __init__(self, send, recv):
        self.send, self.recv, self.count, self.out = send, recv, 0, []

    def copy(self, src, dst, device, landing):
        at = self.count
        self.count += 1

        def describe(a, b):
            return pltpu.make_async_remote_copy(
                src_ref=a,
                dst_ref=b,
                send_sem=self.send.at[at],
                recv_sem=self.recv.at[at],
                device_id=device,
                device_id_type=pl.DeviceIdType.MESH,
            )

        started = describe(src, dst)
        started.start()
        self.out.append(started)
        return describe(landing, landing).wait_recv

    def drain(self):
        for started in self.out:
            started.wait_send()


class Ring:
    def __init__(self, wires, place, half, at, to):
        self.wires, self.place, self.half, self.at, self.to = wires, place, half, at, to
        own = place(at(0))
        self.up = wires.copy(own, own, to[1], place(at(-1)))
        self.down = wires.copy(own, own, to[3], place(at(1)))

    def forward(self):
        far = self.place(self.at(2))
        self.up()
        piece = self.half(self.place(self.at(-1)), 0)
        self.far_up = self.wires.copy(piece, piece, self.to[1], self.half(far, 0))
        self.down()
        piece = self.half(self.place(self.at(1)), 1)
        self.far_down = self.wires.copy(piece, piece, self.to[3], self.half(far, 1))

    def finish(self):
        self.far_up()
        self.far_down()


def kernel(
    grad, m1, m2, l_codes, l_scales, o_codes, o_scales, n_codes, n_scales,
    new_m1, new_m2, update,
    ncode, lcode, o_slab, lb, nb, n2, ob_t, tsend, town, trecv, tz_send, tz_recv, tf,
    mg, wcs, wcr, wys, wyr, wsum, wzs, wzr, wb, w2,
    gsend, gown, grecv, mz_send, mz_recv, mown, df, pf,
    n_sem, l_sem, o_sem, send_sem, recv_sem,
):
    f = lax.axis_index("fsdp")
    r = lax.axis_index("refresh")
    core, y, zh = lax.rem(f, 2), lax.rem(lax.div(f, 2), 4), lax.div(f, 8)
    x, zl = lax.rem(r, 4), lax.div(r, 4)

    def f_at(dz, dy, dc):
        zz = 1 - zh if dz else zh
        cc = 1 - core if dc else core
        return zz * 8 + lax.rem(y + dy + 4, 4) * 2 + cc

    def r_at(dz, dx):
        zz = 1 - zl if dz else zl
        return zz * 4 + lax.rem(x + dx + 4, 4)

    to_x = {d: (f, r_at(0, d)) for d in (1, 2, 3)}
    to_y = {d: (f_at(0, d, 0), r) for d in (1, 2, 3)}
    to_zl, to_zh, to_core = (f, r_at(1, 0)), (f_at(1, 0, 0), r), (f_at(0, 0, 1), r)
    wires = Wires(send_sem, recv_sem)

    def offset(v, unit):
        return pl.multiple_of(v, unit)

    n_jobs = [(z * 2048 + lax.rem(x + d, 4) * RB + h * HB) for h in range(2) for d in (2, 1, 3, 0) for z in range(2)]
    l_jobs = [(z * 2048 + lax.rem(y + d, 4) * RB) for d in (2, 1, 3, 0) for z in range(2)]

    def n_fetch(job):
        return pltpu.make_async_copy(
            n_codes.at[:, pl.ds(offset(n_jobs[job], HB), HB)], ncode.at[job % N_DEPTH], n_sem.at[job % N_DEPTH]
        )

    def l_fetch(job):
        return pltpu.make_async_copy(
            l_codes.at[:, pl.ds(offset(l_jobs[job], RB), RB)], lcode.at[job % L_DEPTH], l_sem.at[job % L_DEPTH]
        )

    o_in = [
        pltpu.make_async_copy(o_codes.at[:, pl.ds(offset(h * 2048 + f * 128, 128), 128)], o_slab.at[h], o_sem.at[h])
        for h in range(2)
    ]
    for c in o_in:
        c.start()
    for job in range(N_DEPTH):
        n_fetch(job).start()
    for job in range(L_DEPTH):
        l_fetch(job).start()

    barrier = pltpu.get_barrier_semaphore()
    friends = [*to_x.values(), *to_y.values(), to_zl, to_zh, to_core]
    for friend in friends:
        pl.semaphore_signal(barrier, inc=1, device_id=friend, device_id_type=pl.DeviceIdType.MESH)

    def widened(scales, group, rows):
        eight = scales[pl.ds(offset(lax.div(group, 8) * 8, 8), 8), rows * 128 : (rows + 1) * 128]
        chosen = lax.broadcasted_iota(jnp.int32, (8, 128), 0) == lax.rem(group, 8)
        row = jnp.sum(jnp.where(chosen, eight, 0.0), axis=0, keepdims=True)
        return jnp.broadcast_to(row, (128, 128)).T

    for h in range(2):
        o_in[h].wait()
        for b in range(4):
            values = (o_slab[h, b * 128 : (b + 1) * 128, :].astype(F32) - 7.5) * widened(o_scales, f + 16 * h, b)
            ob_t[h * 128 : (h + 1) * 128, b * 128 : (b + 1) * 128] = values.T.astype(BF)

    for j in range(2):
        mg[pl.ds(x, 1), j] = (m1, m2)[j][...].astype(BF)[None]

    def expand(slot, scales, out, column, rows, groups):
        for g in range(groups):
            for b in range(rows // 128):
                part = slice(b * 128, (b + 1) * 128)
                v = slot[part, g * 128 : (g + 1) * 128].astype(F32) - 7.5
                v = v * widened(scales, lax.div(column, 128) + g, b)
                out[part, pl.ds(offset(column + g * 128, 128), 128)] = v.astype(BF)

    def n_expand(job):
        n_fetch(job).wait()
        expand(ncode.at[job % N_DEPTH], n_scales, nb, n_jobs[job], RB, 2)
        if job + N_DEPTH < len(n_jobs):
            n_fetch(job + N_DEPTH).start()

    def l_expand(job):
        l_fetch(job).wait()
        expand(lcode.at[job % L_DEPTH], l_scales, lb, l_jobs[job], FB, 4)
        if job + L_DEPTH < len(l_jobs):
            l_fetch(job + L_DEPTH).start()

    mine = pl.ds(offset(core * 256, 256), 256)
    theirs = pl.ds(offset((1 - core) * 256, 256), 256)
    n_waits = []

    def n_swap(h, d):
        within = lax.rem(x + d, 4) * RB + h * HB
        landing = n2.at[mine, pl.ds(offset(within, HB), HB)]
        src = nb.at[mine, pl.ds(offset((1 - zl) * 2048 + within, HB), HB)]
        n_waits.append(wires.copy(src, landing, to_zl, landing))

    t_waits = [[], []]

    def t_part(h):
        for i, d in enumerate((2, 1, 3, 0)):
            for z in range(2):
                job = (h * 4 + i) * 2 + z
                n_expand(job)
                part = dot(ob_t[...], nb[:, pl.ds(offset(n_jobs[job], HB), HB)])
                cols = slice(z * HB, (z + 1) * HB)
                if d:
                    tsend[h, d - 1, :, cols] = part.astype(BF)
                else:
                    town[h, :, cols] = part
            if h == 0 and i == 0:
                pl.semaphore_wait(barrier, len(friends))
            if d:
                t_waits[h].append(wires.copy(tsend.at[h, d - 1], trecv.at[h, d - 1], to_x[d], trecv.at[h, d - 1]))
            n_swap(h, d)

    t_part(0)

    def left_grad(z, d, c):
        lt = lb[:, pl.ds(offset(z * 2048 + lax.rem(y + d, 4) * RB + c * FB, FB), FB)]
        return lax.dot_general(lt, grad[...], (((0,), (0,)), ((), ())), preferred_element_type=F32)

    wc_waits, wy_waits = {}, []

    def send_w(d):
        parts = [left_grad(z, d, core) for z in range(2)]
        wc_waits[d]()
        for z in range(2):
            total = parts[z] + wcr[d, z].astype(F32)
            if d:
                wys[d - 1, z] = total.astype(BF)
            else:
                wsum[z] = total
        if d:
            wy_waits.append(wires.copy(wys.at[d - 1], wyr.at[d - 1], to_y[d], wyr.at[d - 1]))

    before = None
    for i, d in enumerate((2, 1, 3, 0)):
        for z in range(2):
            l_expand(2 * i + z)
            wcs[d, z] = left_grad(z, d, 1 - core).astype(BF)
        wc_waits[d] = wires.copy(wcs.at[d], wcr.at[d], to_core, wcr.at[d])
        if before is not None:
            send_w(before)
        before = d
    send_w(before)

    t_part(1)


    def t_sum(h, z):
        rows = pl.ds(offset(z * 128, 128), 128)
        total = town[h, rows, :]
        for k in range(3):
            total = total + trecv[h, k, rows, :].astype(F32)
        return total

    def t_swap(h):
        for wait in t_waits[h]:
            wait()
        tz_send[h] = t_sum(h, 1 - zl).astype(BF)
        return wires.copy(tz_send.at[h], tz_recv.at[h], to_zl, tz_recv.at[h])

    def t_place(h):
        return lambda i: tf.at[h, pl.ds(offset(i * 128, 128), 128), :]

    def t_own(h):
        tf[h, pl.ds(offset(f * 128, 128), 128), :] = (t_sum(h, zl) + tz_recv[h].astype(F32)).astype(BF)

    def half_of(rows):
        return lambda block, k: block.at[pl.ds(k * rows, rows), :]

    class Spread:
        def __init__(self, place, rows):
            self.place, self.half = place, half_of(rows // 2)
            own = place(f)
            self.z = wires.copy(own, own, to_zh, place(f_at(1, 0, 0)))
            self.e = [wires.copy(own, own, to_core, place(f_at(0, 0, 1)))]

        def pass_core(self, dz, dy):
            block = self.place(f_at(dz, dy, 0))
            self.e.append(wires.copy(block, block, to_core, self.place(f_at(dz, dy, 1))))

        def start(self):
            self.near = Ring(wires, self.place, self.half, lambda d: f_at(0, d, 0), to_y)
            self.z()
            self.other = Ring(wires, self.place, self.half, lambda d: f_at(1, d, 0), to_y)
            self.pass_core(1, 0)

        def forward(self):
            for dz, ring in enumerate((self.near, self.other)):
                ring.forward()
                self.pass_core(dz, 1)
                self.pass_core(dz, -1)

        def finish(self):
            for dz, ring in enumerate((self.near, self.other)):
                ring.finish()
                self.pass_core(dz, 2)
            for wait in self.e:
                wait()

    tz_wait = t_swap(0)
    tz_wait()
    t_own(0)
    spread_t = [Spread(t_place(0), 128)]
    spread_t[0].start()
    ring_m = Ring(wires, lambda i: mg.at[i], lambda block, k: block.at[k], lambda d: lax.rem(x + d + 4, 4), to_x)
    tz_wait = t_swap(1)

    def w_sum(z):
        total = wsum[z]
        for k in range(3):
            total = total + wyr[k, z].astype(F32)
        return total

    for wait in wy_waits:
        wait()
    wzs[...] = w_sum(1 - zh).astype(BF)
    wz_wait = wires.copy(wzs, wzr, to_zh, wzr)
    tz_wait()
    t_own(1)
    spread_t.append(Spread(t_place(1), 128))
    spread_t[0].forward()
    wz_wait()
    wb[...] = (w_sum(zh) + wzr[...].astype(F32)).astype(BF)
    w2_wait = wires.copy(wb, w2, to_zl, w2)
    spread_t[1].start()
    for wait in n_waits:
        wait()
    n_core_wait = wires.copy(n2.at[mine, :], n2.at[mine, :], to_core, n2.at[theirs, :])
    spread_t[0].finish()
    ring_m.forward()
    spread_t[1].forward()
    w2_wait()
    n_core_wait()

    def rotated(d):
        xx = lax.rem(x + d, 4)
        here = dot(wb[...], nb[:, pl.ds(offset(zl * 2048 + xx * RB, RB), RB)])
        return here + dot(w2[...], n2[:, pl.ds(offset(xx * RB, RB), RB)])

    g_waits = []
    for d in (2, 1, 3):
        gsend[d - 1] = rotated(d).astype(BF)
        g_waits.append(wires.copy(gsend.at[d - 1], grecv.at[d - 1], to_x[d], grecv.at[d - 1]))
    gown[...] = rotated(0)

    def moments(z, h):
        a = jnp.zeros((FB, HB), F32)
        b = jnp.zeros((FB, HB), F32)
        for k in range(4):
            t = tf[h, pl.ds(k * RB, RB), pl.ds(offset(z * HB, HB), HB)]
            a = a + dot(mg[k, 0], t)
            b = b + dot(mg[k, 1], t * t)
        return a, b

    def m_swap(h):
        a, b = moments(1 - zl, h)
        mz_send[h, 0] = a.astype(BF)
        mz_send[h, 1] = b.astype(BF)
        return wires.copy(mz_send.at[h], mz_recv.at[h], to_zl, mz_recv.at[h])

    ring_m.finish()
    mz_waits = [m_swap(0)]
    mown[0, 0], mown[0, 1] = moments(zl, 0)
    spread_t[1].finish()
    mz_waits.append(m_swap(1))
    mown[1, 0], mown[1, 1] = moments(zl, 1)
    for wait in g_waits:
        wait()

    spreads = []
    for c in range(NC):
        h, off = (c * CW) // HB, (c * CW) % HB
        if off == 0:
            mz_waits[h]()
        cols = slice(c * CW, (c + 1) * CW)
        rot = gown[:, cols]
        for k in range(3):
            rot = rot + grecv[k, :, cols].astype(F32)
        first = mown[h, 0, :, off : off + CW] + mz_recv[h, 0, :, off : off + CW].astype(F32)
        second = mown[h, 1, :, off : off + CW] + mz_recv[h, 1, :, off : off + CW].astype(F32)
        a = first_beta * first + (1.0 - first_beta) * rot
        b = second_beta * second + (1.0 - second_beta) * rot * rot
        new_m1[:, cols] = a
        new_m2[:, cols] = b
        bias_first = 1.0 - first_beta**STEP
        bias_second = 1.0 - second_beta**STEP
        direction = (a / bias_first) / (jnp.sqrt(b / bias_second) + epsilon)

        def place(i, c=c):
            return df.at[c, pl.ds(offset(i * FB, FB), FB), :]

        df[c, pl.ds(offset(f * FB, FB), FB), :] = direction.astype(BF)
        spreads.append(Spread(place, FB))

    class Share:
        def __init__(self, place):
            self.place = place
            own = place(r)
            self.z = wires.copy(own, own, to_zl, place(r_at(1, 0)))
            self.near = Ring(wires, place, half_of(FB // 2), lambda d: r_at(0, d), to_x)

        def start(self):
            self.z()
            self.other = Ring(wires, self.place, half_of(FB // 2), lambda d: r_at(1, d), to_x)

        def forward(self):
            self.near.forward()
            self.other.forward()

        def finish(self):
            self.near.finish()
            self.other.finish()

    def update_part(c):
        total = jnp.zeros((FB, RB), F32)
        for i in range(8):
            n = nb[:, i * RB + c * CW : i * RB + (c + 1) * CW]
            total = total + lax.dot_general(pf[c, i], n, (((1,), (1,)), ((), ())), preferred_element_type=F32)
        if c == 0:
            update[...] = total
        else:
            update[...] += total

    shares = []
    spreads[0].start()
    spreads[1].start()
    spreads[0].forward()
    for c in range(NC):
        if c + 2 < NC:
            spreads[c + 2].start()
        if c + 1 < NC:
            spreads[c + 1].forward()
        if c >= 1:
            shares[c - 1].start()
        spreads[c].finish()
        pf[c, r] = dot(lb[...], df[c]).astype(BF)
        shares.append(Share(lambda i, c=c: pf.at[c, i]))
        if c >= 1:
            shares[c - 1].forward()
        if c >= 2:
            shares[c - 2].finish()
            update_part(c - 2)
    shares[NC - 1].start()
    shares[NC - 2].finish()
    update_part(NC - 2)
    shares[NC - 1].forward()
    shares[NC - 1].finish()
    update_part(NC - 1)
    wires.drain()


WIRES = 6 + 9 + 4 + 3 + 2 + 2 + 2 * 17 + 4 + 3 + 2 + NC * (17 + 9)


def hand_over(*refs):
    for given, result in zip(refs[:3], refs[3:]):
        result[...] = given[...]


def body(
    grad, exp_avg, exp_avg_sq, left_codes, left_scales,
    right_old_codes, right_old_scales, right_new_codes, right_new_scales,
):
    vmem = pl.BlockSpec(memory_space=pltpu.VMEM)
    hbm = pl.BlockSpec(memory_space=pl.ANY)
    out = jax.ShapeDtypeStruct((FB, RB), F32)
    scratch = [
        pltpu.VMEM((N_DEPTH, RB, HB), jnp.int32),
        pltpu.VMEM((L_DEPTH, FB, RB), jnp.int32),
        pltpu.VMEM((2, RB, 128), jnp.int32),
        pltpu.VMEM((FB, N), BF),
        pltpu.VMEM((RB, N), BF),
        pltpu.VMEM((RB, N // 2), BF),
        pltpu.VMEM((256, RB), BF),
        pltpu.VMEM((2, 3, 256, RB), BF),
        pltpu.VMEM((2, 256, RB), F32),
        pltpu.VMEM((2, 3, 256, RB), BF),
        pltpu.VMEM((2, 128, RB), BF),
        pltpu.VMEM((2, 128, RB), BF),
        pltpu.VMEM((2, N // 2, RB), BF),
        pltpu.VMEM((4, 2, FB, RB), BF),
        pltpu.VMEM((4, 2, FB, RB), BF),
        pltpu.VMEM((4, 2, FB, RB), BF),
        pltpu.VMEM((3, 2, FB, RB), BF),
        pltpu.VMEM((3, 2, FB, RB), BF),
        pltpu.VMEM((2, FB, RB), F32),
        pltpu.VMEM((FB, RB), BF),
        pltpu.VMEM((FB, RB), BF),
        pltpu.VMEM((FB, RB), BF),
        pltpu.VMEM((FB, RB), BF),
        pltpu.VMEM((3, FB, RB), BF),
        pltpu.VMEM((FB, RB), F32),
        pltpu.VMEM((3, FB, RB), BF),
        pltpu.VMEM((2, 2, FB, HB), BF),
        pltpu.VMEM((2, 2, FB, HB), BF),
        pltpu.VMEM((2, 2, FB, HB), F32),
        pltpu.VMEM((NC, N, CW), BF),
        pltpu.VMEM((NC, 8, FB, CW), BF),
        pltpu.SemaphoreType.DMA((N_DEPTH,)),
        pltpu.SemaphoreType.DMA((L_DEPTH,)),
        pltpu.SemaphoreType.DMA((2,)),
        pltpu.SemaphoreType.DMA((WIRES,)),
        pltpu.SemaphoreType.DMA((WIRES,)),
    ]
    results = pl.pallas_call(
        kernel,
        out_shape=(out, out, out),
        in_specs=[vmem, vmem, vmem, hbm, vmem, hbm, vmem, hbm, vmem],
        out_specs=(vmem, vmem, vmem),
        scratch_shapes=scratch,
        compiler_params=pltpu.CompilerParams(
            collective_id=0, has_side_effects=True, vmem_limit_bytes=62 * 2**20
        ),
    )(
        grad, exp_avg, exp_avg_sq, left_codes, left_scales.T,
        right_old_codes, right_old_scales.T, right_new_codes, right_new_scales.T,
    )
    return pl.pallas_call(
        hand_over,
        out_shape=(out, out, out),
        in_specs=[vmem] * 3,
        out_specs=(vmem,) * 3,
    )(*results)


def solution(mesh):
    return jax.shard_map(
        body,
        mesh=mesh,
        in_specs=(
            P("fsdp", "refresh"),
            P("fsdp", "refresh"),
            P("fsdp", "refresh"),
            P("fsdp", None),
            P("fsdp", None),
            P("refresh", None),
            P("refresh", None),
            P("refresh", None),
            P("refresh", None),
        ),
        out_specs=(P("fsdp", "refresh"), P("fsdp", "refresh"), P("fsdp", "refresh")),
        check_vma=False,
    )
```
